512 devices in a mesh: dp: 64 (over y, z), segment: 2 (over core), mp: 4 (over x).
Axes of the slice: x: 4, y: 4, z: 16, core: 2. Of those that a mesh axis runs over, the one named last changes fastest.
Arguments:
- hidden: bfloat16 [2, 512, 4096], P('segment', ('dp', 'mp')), may hold values from -6 to 6
- gain: float32 [4096], replicated, may hold values from 0.5 to 1.5
- head: bfloat16 [4096, 131072], P('segment', ('dp', 'mp')), may hold values from -0.09375 to 0.09375
- queries: bfloat16 [8, 131072], P(None, ('dp', 'mp')), may hold values from -48 to 48
- doc_spans: int32 [8], replicated, may hold values from 1 to 4, as said below
- labels: int32 [8], replicated, may hold values from 0 to 7
Outputs:
- grad_head: bfloat16 [4096, 131072], P('segment', ('dp', 'mp'))
- loss: float32 [], replicated
The draws below stay inside these ranges and needn't reach their ends.
Inputs may be any that keep to these rules, and one draw needn't show every extreme that they name: `doc_spans`: the counts sum to 16; documents own consecutive spans in order; at least two documents have 4 spans.
All inputs are finite; a program needn't handle non-finite values.
Results may differ from the reference program's by a relative error of at most 0.008.
Values may be sent and summed in bfloat16 or wider, within the bound.
A program may use at most 64 MiB of HBM per device.

```python
import math
import jax
import jax.numpy as jnp
from jax import lax

D = 4096
V_DEV = 512
CH_MB = 8
NDOC = 8
NQ = 8
MOST = 4
MICRO = 2
VOCAB = 131072
TOK_MB = 512
SPAN = 64
TOKENS = 1024


def draw_queries(key, part):
    drawn = jnp.clip(jax.random.normal(key, (NQ, VOCAB), jnp.float32), -6.0, 6.0)
    return drawn.astype(jnp.bfloat16)


def draw_doc_spans(key, part):
    total = MICRO * CH_MB
    remaining = total - 2 * MOST - (NDOC - 2)
    spare_slots = (NDOC - 2) * (MOST - 1)
    slot_order = jax.random.permutation(jax.random.fold_in(key, 11), spare_slots)
    owners = slot_order[:remaining] // (MOST - 1)
    extras = jnp.sum((owners[:, None] == jnp.arange(NDOC - 2, dtype=jnp.int32)[None, :]).astype(jnp.int32), axis=0)
    ranked = jnp.concatenate([jnp.full((2,), MOST, jnp.int32), 1 + extras.astype(jnp.int32)])
    doc_order = jax.random.permutation(jax.random.fold_in(key, 13), NDOC)
    return jnp.zeros((NDOC,), jnp.int32).at[doc_order].set(ranked)


def place_ends(values, stream_key, least, high):
    index_at = [jax.random.randint(jax.random.fold_in(stream_key, axis), (), 0, length) for axis, length in enumerate(values.shape)]
    widest = values.shape.index(max(values.shape))
    beside = index_at[:widest] + [(index_at[widest] + 1) % values.shape[widest]] + index_at[widest + 1:]
    return values.at[tuple(index_at)].set(least).at[tuple(beside)].set(high)


def level_of(stream_key, extent, shards, low, high):
    level = 1.0
    for axis_at, parts in shards:
        steps = jax.random.uniform(jax.random.fold_in(jax.random.fold_in(stream_key, 6), axis_at), (parts,), jnp.float32, low / len(shards), high / len(shards))
        level = level * jnp.repeat(jnp.exp(steps), extent[axis_at] // parts).reshape((-1,) + (1,) * (len(extent) - 1 - axis_at))
    return level


def bell_draw(rng, extent, deviation, most, split=(), kind=jnp.bfloat16):
    level = level_of(rng, extent, split, -0.22, 0.18) if split else 1.0
    entries = jax.random.normal(rng, extent, jnp.float32) * deviation * level
    return jnp.minimum(jnp.maximum(entries, -most), most).astype(kind)


def setup_inputs(seed: int = 0) -> dict:
    seeds = jax.random.split(jax.random.key(seed), 7)
    hidden = bell_draw(seeds[0], (MICRO, TOK_MB, D), 1.0, 6.0, ((0, 2), (1, 256)))
    gain = jnp.clip(1.0 + 0.1 * jax.random.normal(seeds[1], (D,), jnp.float32), 0.5, 1.5)
    head = bell_draw(seeds[2], (D, VOCAB), D ** -0.5, 0.09375, ((0, 2), (1, 256)))
    queries = draw_queries(jax.random.fold_in(seeds[6], 71), 0)
    doc_spans = draw_doc_spans(jax.random.fold_in(seeds[6], 71), 0)
    labels = place_ends(jax.random.randint(seeds[5], (NQ,), 0, NDOC), jax.random.fold_in(seeds[5], 1), 0, NDOC - 1).astype(jnp.int32)
    return {"hidden": hidden, "gain": gain, "head": head, "queries": queries, "doc_spans": doc_spans, "labels": labels}


def saturate(logits):
    return jnp.log1p(jax.nn.softplus(logits))

def slope(logits):
    return jax.nn.sigmoid(logits) / (1.0 + jax.nn.softplus(logits))

def reference(hidden, gain, head, queries, doc_spans, labels):
    bounds = jnp.concatenate([jnp.zeros((1,), jnp.int32), jnp.cumsum(doc_spans).astype(jnp.int32)])
    span_ids = jnp.arange(TOKENS, dtype=jnp.int32) // SPAN
    table = ((span_ids[:, None] >= bounds[None, :-1]) & (span_ids[:, None] < bounds[None, 1:])).astype(jnp.float32)
    values = hidden.astype(jnp.float32).reshape(TOKENS, D)
    mean_sq = lax.optimization_barrier(jnp.mean(values * values, axis=-1, keepdims=True))
    normed = (values * lax.rsqrt(mean_sq + 1e-05) * gain).astype(jnp.bfloat16)
    scale = 1.0 / (math.sqrt(VOCAB) * SPAN)
    grad_scale = math.sqrt(VOCAB) * SPAN / math.sqrt(TOKENS)
    blocks = jnp.arange(VOCAB // V_DEV, dtype=jnp.int32)

    def forward(total, block):
        weights = lax.dynamic_slice_in_dim(head, block * V_DEV, V_DEV, 1)
        query_block = lax.dynamic_slice_in_dim(queries, block * V_DEV, V_DEV, 1).astype(jnp.float32)
        logits = jnp.dot(normed, weights, preferred_element_type=jnp.float32)
        pooled = jnp.dot(table.T, saturate(logits), precision=lax.Precision.HIGHEST)
        return (total + jnp.dot(query_block, pooled.T, precision=lax.Precision.HIGHEST), None)
    total, _ = lax.scan(forward, jnp.zeros((NQ, NDOC), jnp.float32), blocks)
    scores = total * scale
    row_top = lax.optimization_barrier(jnp.max(scores, axis=1, keepdims=True))
    log_total = row_top + jnp.log(lax.optimization_barrier(jnp.sum(jnp.exp(scores - row_top), axis=1, keepdims=True)))
    picks = (labels[:, None] == jnp.arange(NDOC, dtype=jnp.int32)[None, :]).astype(jnp.float32)
    loss = jnp.sum(log_total[:, 0] - lax.optimization_barrier(jnp.sum(scores * picks, axis=1)))
    score_grad = jnp.exp(scores - log_total) - picks

    def backward(carry, block):
        weights = lax.dynamic_slice_in_dim(head, block * V_DEV, V_DEV, 1)
        query_block = lax.dynamic_slice_in_dim(queries, block * V_DEV, V_DEV, 1).astype(jnp.float32)
        pooled_grad = scale * jnp.dot(score_grad.T, query_block, precision=lax.Precision.HIGHEST)
        logits = jnp.dot(normed, weights, preferred_element_type=jnp.float32)
        token_grad = jnp.dot(table, pooled_grad, precision=lax.Precision.HIGHEST)
        logit_grad = (token_grad * slope(logits) * grad_scale).astype(jnp.bfloat16)
        summed = jnp.zeros((D, V_DEV), jnp.float32)
        for micro_batch in range(MICRO):
            rows = normed[micro_batch * TOK_MB:(micro_batch + 1) * TOK_MB]
            grads = logit_grad[micro_batch * TOK_MB:(micro_batch + 1) * TOK_MB]
            part = lax.optimization_barrier(jnp.dot(rows.T, grads, preferred_element_type=jnp.float32).astype(jnp.bfloat16))
            summed = summed + part.astype(jnp.float32)
        return (carry, summed.astype(jnp.bfloat16))
    _, pieces = lax.scan(backward, jnp.zeros((), jnp.float32), blocks)
    grad_head = jnp.transpose(pieces, (1, 0, 2)).reshape(D, VOCAB)
    return (grad_head, loss)
```

```python
import functools
import math

import jax
import jax.numpy as jnp
from jax import lax
from jax.experimental import pallas as pl
from jax.experimental.pallas import tpu as pltpu
from jax.sharding import PartitionSpec as P

MESH = pl.DeviceIdType.MESH
NX, NY, NZ = 4, 4, 16
V_DEV = 512
NDOC = 8
NQ = 8
SPANS = 16
SPAN = 64
VOCAB = 131072
TOKENS = 1024
D = 4096
DH = D // 2
LANES = 128

WA, WB, WQ = 768, 768, 128
A_CHUNKS = ((0, 384), (384, 384))
B_AT, B_WIDTH = WA, WB + WQ
B_HALVES = ((WA, 512), (WA + 512, B_WIDTH - 512))
C_AT = WA + WB
assert C_AT + 4 * WQ == DH

LAST = 11


def wrap(i, n):
    return lax.rem(i + 2 * n, n)


def kernel(
    hidden, gain, head, queries, doc_spans, labels,
    out, loss,
    ysend, yland, xs, hs, mine, sent, got, slopes, pool, xt, lg, outs, spg,
    ar0, ar1, ar2, ar3,
    h_sem, o_sem,
    p1_s, p1_r, y_s, y_r, rb_s, rb_r, ra_s, ra_r, x_s, x_r, pp_s, pp_r, sl_s, sl_r,
    a1_s, a1_r, a2_s, a2_r, a3_s, a3_r,
):
    x = lax.axis_index("mp")
    s = lax.axis_index("segment")
    dp = lax.axis_index("dp")
    y = dp // NZ
    z = lax.rem(dp, NZ)

    def dev(dx=0, dy=0, dz=0, ds=0):
        return (
            wrap(y + dy, NY) * NZ + wrap(z + dz, NZ),
            wrap(s + ds, 2),
            wrap(x + dx, NX),
        )

    def copy(src, dst, s_sem, r_sem, device):
        return pltpu.make_async_remote_copy(
            src, dst, s_sem, r_sem, device, device_id_type=MESH
        )

    near = [(dx, ds) for dx in range(NX) for ds in range(2) if dx or ds]
    barrier = pltpu.get_barrier_semaphore()
    peers = [dev(dx=dx, ds=ds) for dx, ds in near]
    peers += [dev(dy=dy) for dy in range(1, NY)]
    peers += [dev(dz=1), dev(dz=-1)]
    for p in peers:
        pl.semaphore_signal(barrier, inc=1, device_id=p, device_id_type=MESH)

    def h_copies():
        yield pltpu.make_async_copy(head.at[pl.ds(0, C_AT)], hs.at[pl.ds(0, C_AT)], h_sem.at[0])
        for r in range(NX):
            at = pl.multiple_of(C_AT + wrap(x + r, NX) * WQ, WQ)
            yield pltpu.make_async_copy(
                head.at[pl.ds(at, WQ)], hs.at[pl.ds(C_AT + r * WQ, WQ)], h_sem.at[1 + r]
            )

    for c in h_copies():
        c.start()

    values = hidden[0].astype(jnp.float32)
    mean_sq = jnp.mean(values * values, axis=-1, keepdims=True)
    normed = (values * lax.rsqrt(mean_sq + 1e-05) * gain[...]).astype(jnp.bfloat16)
    normed = normed.astype(jnp.float32)
    for k in range(D // LANES):
        ysend[k // 16, :, k % 16, :] = normed[:, k * LANES : (k + 1) * LANES]
    pool[...] = jnp.zeros_like(pool)

    pl.semaphore_wait(barrier, len(peers))

    def p1(i, dx, ds, landing):
        return copy(
            ysend.at[wrap(s + ds, 2)],
            yland.at[pl.ds(landing * 2, 2)],
            p1_s.at[i], p1_r.at[i], dev(dx=dx, ds=ds),
        )

    for i, (dx, ds) in enumerate(near):
        p1(i, dx, ds, s * NX + x).start()
    yland[pl.ds((s * NX + x) * 2, 2)] = ysend[s]
    for i, (dx, ds) in enumerate(near):
        p1(i, dx, ds, wrap(s + ds, 2) * NX + wrap(x - dx, NX)).wait_recv()
    for k in range(C_AT // LANES):
        xs[z, y, :, k * LANES : (k + 1) * LANES] = yland[:, k, :].astype(jnp.bfloat16)
    for xx in range(NX):

        @pl.when(x == xx)
        def _():
            for r in range(NX):
                k = C_AT // LANES + (xx + r) % NX
                at = C_AT + r * WQ
                xs[z, y, :, at : at + WQ] = yland[:, k, :].astype(jnp.bfloat16)

    def zed(k, d):
        return wrap(z - k, NZ) if d == 0 else wrap(z + k, NZ)

    def ring_b(k, d, zb, at=B_AT, width=B_WIDTH):
        ref = xs.at[zb, y, :, pl.ds(at, width)]
        return copy(ref, ref, rb_s.at[d, k], rb_r.at[d, k], dev(dz=1 - 2 * d))

    def ring_a(k, d, c, zb):
        ref = xs.at[zb, :, :, pl.ds(*A_CHUNKS[c])]
        return copy(ref, ref, ra_s.at[d, k, c], ra_r.at[d, k, c], dev(dz=1 - 2 * d))

    def relay_y(i, dy, zb, yb, at=B_AT, width=B_WIDTH):
        ref = xs.at[zb, yb, :, pl.ds(at, width)]
        return copy(ref, ref, y_s.at[i, dy - 1], y_r.at[i, dy - 1], dev(dy=dy))

    def relay_x(i, dx, zb):
        return copy(
            xs.at[zb, :, :, pl.ds(C_AT, WQ)],
            xs.at[zb, :, :, pl.ds(C_AT + (NX - dx) * WQ, WQ)],
            x_s.at[i, dx - 1], x_r.at[i, dx - 1], dev(dx=dx),
        )

    def partial(k):
        return copy(sent.at[k], got.at[k], pp_s.at[k], pp_r.at[k], dev(ds=1))

    def zown(k):
        return lax.rem(z + jnp.where(s == 0, NZ - k, k), NZ)

    def zother(k):
        return lax.rem(z + jnp.where(s == 0, k, NZ - k), NZ)

    def slope_copy(k, zb):
        return copy(slopes.at[zb], slopes.at[zb], sl_s.at[k], sl_r.at[k], dev(ds=1))

    def rows_of(zb):
        return xs[zb].reshape(NY * 16, DH)

    for d in range(2):
        ring_b(1, d, z).start()
    for dy in range(1, NY):
        relay_y(0, dy, z, y, 0, DH).start()
    for dy in range(1, NY):
        relay_y(0, dy, z, wrap(y - dy, NY), 0, DH).wait_recv()
    for c in range(2):
        for d in range(2):
            ring_a(1, d, c, z).start()
    for c in h_copies():
        c.wait()
    product = jnp.dot(rows_of(z), hs[...], preferred_element_type=jnp.float32)
    mine[0] = product
    sent[0] = product
    partial(0).start()

    def step(k, carry):
        @pl.when(k <= 7)
        def _():
            for d in range(2):
                ring_b(k, d, zed(k, d)).wait_recv()

            @pl.when(k < 7)
            def _():
                for d in range(2):
                    ring_b(k + 1, d, zed(k, d)).start()

            @pl.when(k == 7)
            def _():
                for d in range(2):
                    ring_b(8, d, zed(7, d), *B_HALVES[d]).start()

            for d in range(2):
                for dy in range(1, NY):
                    relay_y(2 * k - 1 + d, dy, zed(k, d), y).start()
            for c in range(2):
                for d in range(2):
                    ring_a(k, d, c, zed(k, d)).wait_recv()

                    @pl.when((k < 7) | (c == d))
                    def _():
                        ring_a(k + 1, d, c, zed(k, d)).start()

        @pl.when(k == 8)
        def _():
            zb = zed(8, 0)
            for d in range(2):
                ring_b(8, d, zb, *B_HALVES[d]).wait_recv()
            for dy in range(1, NY):
                relay_y(15, dy, zb, y).start()
            for d in range(2):
                ring_a(8, d, d, zb).wait_recv()

        @pl.when((k >= 2) & (k <= 9))
        def _():
            j = k - 1
            for d in range(2):

                @pl.when((j <= 7) | (d == 0))
                def _():
                    i = 2 * j - 1 + d
                    zb = zed(j, d)
                    for dy in range(1, NY):
                        relay_y(i, dy, zb, wrap(y - dy, NY)).wait_recv()
                    for dx in range(1, NX):
                        relay_x(i, dx, zb).start()

        @pl.when((k >= 3) & (k <= 9))
        def _():
            j = k - 2
            for d in range(2):
                for dx in range(1, NX):
                    relay_x_wait(2 * j - 1 + d, dx, zed(j, d))
            both = jnp.concatenate([rows_of(zown(j)), rows_of(zother(j))], axis=0)
            product = jnp.dot(both, hs[...], preferred_element_type=jnp.float32)
            mine[j] = product[: NY * 16]
            sent[j] = product[NY * 16 :]
            partial(j).start()

        @pl.when(k == 10)
        def _():
            zb = zed(8, 0)
            for dx in range(1, NX):
                relay_x_wait(15, dx, zb)
            product = jnp.dot(rows_of(zb), hs[...], preferred_element_type=jnp.float32)
            mine[8] = product
            sent[8] = product
            partial(8).start()

        @pl.when(k >= 3)
        def _():
            j = k - 3
            zb = zown(j)
            late = jnp.where(zb >= NZ // 2, 1, 0)
            counts = (j > 0) & (j < 8) | (j == 0) & (s == 0) | (j == 8) & (s == 1)
            weight = jnp.where(counts, 1.0, 0.0).astype(jnp.float32)
            partial(j).wait_recv()
            for yb in range(NY):
                rows = pl.ds(yb * 16, 16)
                logits = mine[j, rows, :] + got[j, rows, :]
                small = jnp.exp(-jnp.abs(logits))
                soft = jnp.maximum(logits, 0.0) + jnp.log1p(small)
                pool[late, yb] += weight * jnp.log1p(soft)
                top = jnp.where(logits >= 0.0, 1.0, small)
                slope = top / ((1.0 + small) * (1.0 + soft))
                slopes[zb, rows, :] = slope.astype(jnp.bfloat16)

            @pl.when((j > 0) & (j < 8))
            def _():
                slope_copy(j, zb).start()

        return carry

    def relay_x_wait(i, dx, zb):
        ref = xs.at[zb, :, :, pl.ds(C_AT + (NX - dx) * WQ, WQ)]
        copy(ref, ref, x_s.at[i, dx - 1], x_r.at[i, dx - 1], dev(dx=dx)).wait_recv()

    lax.fori_loop(1, LAST + 1, step, 0)

    lane = lax.broadcasted_iota(jnp.int32, (NQ, LANES), 1)
    row = lax.broadcasted_iota(jnp.int32, (NQ, LANES), 0)
    query = queries[...].astype(jnp.float32)
    terms = jnp.zeros((NQ, LANES), jnp.float32)
    for late in range(2):
        for yb in range(NY):
            for m in range(2):
                total = jnp.sum(pool[late, yb, m * 8 : (m + 1) * 8, :], axis=0, keepdims=True)
                term = jnp.sum(query * total, axis=1, keepdims=True)
                terms = jnp.where(lane == m * 8 + yb * 2 + late, term, terms)

    def transpose(c, carry):
        at = pl.multiple_of(c * LANES, LANES)
        block = xs[:, :, :, pl.ds(at, LANES)].reshape(TOKENS, LANES)
        xt[pl.ds(at, LANES), :] = block.T
        return carry

    ar0[...] = terms
    to_core = copy(ar0, ar1, a1_s, a1_r, dev(ds=1))
    to_core.start()
    to_core.wait_recv()
    chip = terms + ar1[...]
    ar0_xy = ar2.at[x * NY + y]
    ar2[x * NY + y] = chip

    def to_xy(i):
        return copy(ar0_xy, ar0_xy, a2_s.at[i], a2_r.at[i], dev(dx=i // NY, dy=lax.rem(i, NY)))

    def from_xy(i):
        ref = ar2.at[wrap(x - i // NY, NX) * NY + wrap(y - lax.rem(i, NY), NY)]
        return copy(ref, ref, a2_s.at[i], a2_r.at[i], dev())

    def start_xy(i, carry):
        to_xy(i).start()
        return carry

    def wait_xy(i, carry):
        from_xy(i).wait_recv()
        return carry

    lax.fori_loop(1, NX * NY, start_xy, 0)
    lax.fori_loop(0, 6, transpose, 0)
    lax.fori_loop(1, NX * NY, wait_xy, 0)
    plane = jnp.zeros((NQ, LANES), jnp.float32)
    for i in range(NX * NY):
        plane += ar2[i]
    ar3[z] = plane
    ar_z = ar3.at[z]

    def to_z(i):
        return copy(ar_z, ar_z, a3_s.at[i], a3_r.at[i], dev(dz=i))

    def from_z(i):
        ref = ar3.at[wrap(z - i, NZ)]
        return copy(ref, ref, a3_s.at[i], a3_r.at[i], dev())

    def start_z(i, carry):
        to_z(i).start()
        return carry

    def wait_z(i, carry):
        from_z(i).wait_recv()
        return carry

    lax.fori_loop(1, NZ, start_z, 0)
    lax.fori_loop(6, DH // LANES, transpose, 0)

    def wait_step(k, carry):
        slope_copy(k, zother(k)).wait_recv()
        slope_copy(k, zown(k)).wait_send()
        for d in range(2):
            ring_b(k, d, z).wait_send()
            for c in range(2):
                ring_a(k, d, c, z).wait_send()
            for o in range(1, NY):
                relay_y(2 * k - 1 + d, o, z, y).wait_send()
                relay_x(2 * k - 1 + d, o, z).wait_send()
        partial(k).wait_send()
        return carry

    lax.fori_loop(1, 8, wait_step, 0)
    for d in range(2):
        ring_b(8, d, z, *B_HALVES[d]).wait_send()
        ring_a(8, d, d, z).wait_send()
    for o in range(1, NY):
        relay_y(0, o, z, y, 0, DH).wait_send()
        relay_y(15, o, z, y).wait_send()
        relay_x(15, o, z).wait_send()
    partial(0).wait_send()
    partial(8).wait_send()
    for i, (dx, ds) in enumerate(near):
        p1(i, dx, ds, 0).wait_send()
    to_core.wait_send()

    def sent_xy(i, carry):
        to_xy(i).wait_send()
        return carry

    lax.fori_loop(1, NX * NY, sent_xy, 0)
    lax.fori_loop(1, NZ, wait_z, 0)
    whole = jnp.zeros((NQ, LANES), jnp.float32)
    for i in range(NZ):
        whole += ar3[i]

    masks = []
    first = jnp.int32(0)
    scores = jnp.zeros((NQ, LANES), jnp.float32)
    for d in range(NDOC):
        after = first + doc_spans[d]
        masks.append((lane >= first) & (lane < after))
        term = jnp.sum(jnp.where(masks[d], whole, 0.0), axis=1, keepdims=True)
        scores = jnp.where(lane == d, term, scores)
        first = after
    scores = scores * (1.0 / (math.sqrt(VOCAB) * SPAN))
    valid = lane < NDOC
    row_top = jnp.max(jnp.where(valid, scores, -jnp.inf), axis=1, keepdims=True)
    total = jnp.sum(jnp.where(valid, jnp.exp(scores - row_top), 0.0), axis=1, keepdims=True)
    log_total = row_top + jnp.log(total)
    picks = jnp.zeros((NQ, LANES), jnp.float32)
    for q in range(NQ):
        picks = jnp.where((row == q) & (lane == labels[q]), 1.0, picks)
    picked = jnp.sum(scores * picks, axis=1, keepdims=True)
    loss[...] = jnp.sum(log_total - picked, axis=0, keepdims=True)
    grad = jnp.where(valid, jnp.exp(scores - log_total), 0.0) - picks
    grad = grad * (1.0 / math.sqrt(TOKENS))
    by_span = jnp.zeros((NQ, LANES), jnp.float32)
    for d in range(NDOC):
        column = jnp.sum(jnp.where(lane == d, grad, 0.0), axis=1, keepdims=True)
        by_span = jnp.where(masks[d], column, by_span)
    for i in range(SPANS):
        spg[i : i + 1, :] = jnp.sum(by_span[:, i : i + 1] * query, axis=0, keepdims=True)

    for late in range(2):

        def to_lg(k, carry, late=late):
            zb = late * (NZ // 2) + k
            for yb in range(NY):
                slope = slopes[zb, yb * 16 : (yb + 1) * 16, :].astype(jnp.float32)
                parts = [
                    slope[m * 8 : (m + 1) * 8] * spg[m * 8 + yb * 2 + late, :][None, :]
                    for m in range(2)
                ]
                at = pl.multiple_of(zb * 64 + yb * 16, 16)
                lg[pl.ds(at, 16), :] = jnp.concatenate(parts, axis=0).astype(jnp.bfloat16)
            return carry

        lax.fori_loop(0, NZ // 2, to_lg, 0)

    def out_copy(b):
        quarter = C_AT // WQ + wrap(x + b, NX)
        at = pl.multiple_of(jnp.where(b < C_AT // WQ, b, quarter) * WQ, WQ)
        here = pl.multiple_of(b * WQ, WQ)
        return pltpu.make_async_copy(outs.at[pl.ds(here, WQ)], out.at[pl.ds(at, WQ)], o_sem.at[b])

    tile = 256

    def to_out(t, carry):
        at = pl.ds(pl.multiple_of(t * tile, tile), tile)
        block = jnp.dot(xt[at, :], lg[...], preferred_element_type=jnp.float32)
        outs[at, :] = block.astype(jnp.bfloat16)
        for h in range(tile // WQ):
            out_copy(t * (tile // WQ) + h).start()
        return carry

    lax.fori_loop(0, DH // tile, to_out, 0)

    def sent_z(i, carry):
        to_z(i).wait_send()
        return carry

    lax.fori_loop(1, NZ, sent_z, 0)

    def out_wait(b, carry):
        out_copy(b).wait()
        return carry

    lax.fori_loop(0, DH // WQ, out_wait, 0)


def shards(hidden, gain, head, queries, doc_spans, labels):
    dma = pltpu.SemaphoreType.DMA
    f32, bf16 = jnp.float32, jnp.bfloat16
    vmem = pl.BlockSpec(memory_space=pltpu.VMEM)
    smem = pl.BlockSpec(memory_space=pltpu.SMEM)
    hbm = pl.BlockSpec(memory_space=pl.ANY)
    grad_head, loss = pl.pallas_call(
        kernel,
        name="splade_head",
        out_shape=(
            jax.ShapeDtypeStruct((DH, V_DEV), bf16),
            jax.ShapeDtypeStruct((1, 1), f32),
        ),
        in_specs=[vmem, vmem, hbm, vmem, smem, smem],
        out_specs=(hbm, vmem),
        scratch_shapes=[
            pltpu.VMEM((2, 2, 16, LANES), f32),
            pltpu.VMEM((16, 16, LANES), f32),
            pltpu.VMEM((NZ, NY, 16, DH), bf16),
            pltpu.VMEM((DH, V_DEV), bf16),
            pltpu.VMEM((9, NY * 16, V_DEV), f32),
            pltpu.VMEM((9, NY * 16, V_DEV), f32),
            pltpu.VMEM((9, NY * 16, V_DEV), f32),
            pltpu.VMEM((NZ, NY * 16, V_DEV), bf16),
            pltpu.VMEM((2, NY, 16, V_DEV), f32),
            pltpu.VMEM((DH, TOKENS), bf16),
            pltpu.VMEM((TOKENS, V_DEV), bf16),
            pltpu.VMEM((DH, V_DEV), bf16),
            pltpu.VMEM((SPANS, V_DEV), f32),
            pltpu.VMEM((NQ, LANES), f32),
            pltpu.VMEM((NQ, LANES), f32),
            pltpu.VMEM((NX * NY, NQ, LANES), f32),
            pltpu.VMEM((NZ, NQ, LANES), f32),
            dma((5,)), dma((DH // WQ,)),
            dma((7,)), dma((7,)),
            dma((16, 3)), dma((16, 3)),
            dma((2, 9)), dma((2, 9)),
            dma((2, 9, 2)), dma((2, 9, 2)),
            dma((16, 3)), dma((16, 3)),
            dma((9,)), dma((9,)),
            dma((9,)), dma((9,)),
            dma, dma,
            dma((16,)), dma((16,)),
            dma((16,)), dma((16,)),
        ],
        compiler_params=pltpu.CompilerParams(
            collective_id=0, has_side_effects=True, vmem_limit_bytes=48 * 2**20
        ),
    )(hidden, gain.reshape(1, D), head, queries, doc_spans, labels)
    return (grad_head, loss.reshape(()))


def solution(mesh):
    return jax.shard_map(
        shards,
        mesh=mesh,
        in_specs=(
            P("segment", ("dp", "mp"), None),
            P(),
            P("segment", ("dp", "mp")),
            P(None, ("dp", "mp")),
            P(),
            P(),
        ),
        out_specs=(P("segment", ("dp", "mp")), P()),
        check_vma=False,
    )
```

```python
import functools
import math

import jax
import jax.numpy as jnp
from jax import lax
from jax.experimental import pallas as pl
from jax.experimental.pallas import tpu as pltpu
from jax.sharding import PartitionSpec as P

MESH = pl.DeviceIdType.MESH
NX, NY, NZ = 4, 4, 16
V_DEV = 512
NDOC = 8
NQ = 8
SPANS = 16
ROWS = 128
SPAN = 64
VOCAB = 131072
TOKENS = 1024
D = 4096
DH = D // 2
LANES = 128

WB, WQ = 1024, 256
WHOLE = (0, WB + WQ)
HALVES = ((0, 640), (640, WB + WQ - 640))
C_AT = WB
assert C_AT + 4 * WQ == DH

OWN = 15
STEPS = 4


def wrap(i, n):
    return lax.rem(i + 2 * n, n)


def kernel(
    hidden_at, gain_at, head, queries_at, doc_spans_at, labels_at,
    out, loss,
    hidden, gain, queries, doc_spans, labels,
    ysend, yland, xs, hs, mine, sent, got, slopes, pool, xt, lg, outs, spg,
    ar0, ar1, ar2, ar3,
    in_sem, h_sem, o_sem,
    p1_s, p1_r, y_s, y_r, r_s, r_r, x_s, x_r, pp_s, pp_r, sl_s, sl_r,
    a1_s, a1_r, a2_s, a2_r, a3_s, a3_r,
):
    x = lax.axis_index("mp")
    s = lax.axis_index("segment")
    dp = lax.axis_index("dp")
    y = dp // NZ
    z = lax.rem(dp, NZ)

    def dev(dx=0, dy=0, dz=0, ds=0):
        return (
            wrap(y + dy, NY) * NZ + wrap(z + dz, NZ),
            wrap(s + ds, 2),
            wrap(x + dx, NX),
        )

    def copy(src, dst, s_sem, r_sem, device):
        return pltpu.make_async_remote_copy(
            src, dst, s_sem, r_sem, device, device_id_type=MESH
        )

    inputs = [
        pltpu.make_async_copy(a, b, in_sem.at[i])
        for i, (a, b) in enumerate(
            ((hidden_at, hidden), (gain_at, gain), (queries_at, queries),
             (doc_spans_at, doc_spans), (labels_at, labels))
        )
    ]
    for c in inputs:
        c.start()

    near = [(dx, ds) for dx in range(NX) for ds in range(2) if dx or ds]
    barrier = pltpu.get_barrier_semaphore()
    peers = [dev(dx=dx, ds=ds) for dx, ds in near]
    peers += [dev(dy=dy) for dy in range(1, NY)]
    peers += [dev(dz=dz) for dz in (1, 2, -1, -2)]
    for p in peers:
        pl.semaphore_signal(barrier, inc=1, device_id=p, device_id_type=MESH)

    h_copies = [pltpu.make_async_copy(head.at[pl.ds(0, C_AT)], hs.at[pl.ds(0, C_AT)], h_sem.at[0])]
    for r in range(NX):
        at = pl.multiple_of(C_AT + wrap(x + r, NX) * WQ, WQ)
        h_copies.append(
            pltpu.make_async_copy(
                head.at[pl.ds(at, WQ)], hs.at[pl.ds(C_AT + r * WQ, WQ)], h_sem.at[1 + r]
            )
        )

    inputs[0].wait()
    inputs[1].wait()
    values = hidden[0].astype(jnp.float32)
    mean_sq = jnp.mean(values * values, axis=-1, keepdims=True)
    normed = (values * lax.rsqrt(mean_sq + 1e-05) * gain[...]).astype(jnp.bfloat16)
    normed = normed.astype(jnp.float32)
    for k in range(D // LANES):
        ysend[k // 16, :, k % 16, :] = normed[:, k * LANES : (k + 1) * LANES]

    pl.semaphore_wait(barrier, len(peers))

    def p1(i, dx, ds, landing):
        return copy(
            ysend.at[wrap(s + ds, 2)],
            yland.at[pl.ds(landing * 2, 2)],
            p1_s.at[i], p1_r.at[i], dev(dx=dx, ds=ds),
        )

    for i, (dx, ds) in enumerate(near):
        p1(i, dx, ds, s * NX + x).start()
    for c in h_copies:
        c.start()
    yland[pl.ds((s * NX + x) * 2, 2)] = ysend[s]
    pool[...] = jnp.zeros_like(pool)
    for i, (dx, ds) in enumerate(near):
        p1(i, dx, ds, wrap(s + ds, 2) * NX + wrap(x - dx, NX)).wait_recv()
    for k in range(C_AT // LANES):
        xs[OWN, y, :, k * LANES : (k + 1) * LANES] = yland[:, k, :].astype(jnp.bfloat16)
    for xx in range(NX):

        @pl.when(x == xx)
        def _():
            for r in range(NX):
                for h in range(WQ // LANES):
                    k = (C_AT + (xx + r) % NX * WQ) // LANES + h
                    at = C_AT + r * WQ + h * LANES
                    xs[OWN, y, :, at : at + LANES] = yland[:, k, :].astype(jnp.bfloat16)

    def ring_copy(k, d, piece, src, dst, n, hops, columns=WHOLE):
        a, b = (xs.at[pl.ds(i, n), y, :, pl.ds(*columns)] for i in (src, dst))
        at = 4 * k + 2 * d + piece
        return copy(a, b, r_s.at[at], r_r.at[at], dev(dz=hops if d == 0 else -hops))

    def ring_first(d):
        return [ring_copy(1, d, i, OWN, 8 * d + i, 1, 1 + i) for i in range(2)]

    def ring_middle(d, k):
        at = 8 * d + 2 * (k - 1)
        return [ring_copy(k, d, 0, at - 2, at, 2, 2)]

    def ring_last(d):
        return [
            ring_copy(STEPS, d, 0, 8 * d + 4, 8 * d + 6, 1, 2),
            ring_copy(STEPS, d, 1, 8 * d + 5, 7, 1, 2, HALVES[d]),
        ]

    def start(copies):
        for c in copies:
            c.start()

    def arrive(copies):
        for c in copies:
            c.wait_recv()

    def own_y(dy, yb):
        ref = xs.at[OWN, yb]
        return copy(ref, ref, y_s.at[0, dy - 1], y_r.at[0, dy - 1], dev(dy=dy))

    def relay_y(i, dy, slot, n, yb):
        ref = xs.at[pl.ds(slot, n), yb, :, pl.ds(*WHOLE)]
        return copy(ref, ref, y_s.at[i, dy - 1], y_r.at[i, dy - 1], dev(dy=dy))

    def relay_x(i, dx, slot, n):
        return copy(
            xs.at[pl.ds(slot, n), :, :, pl.ds(C_AT, WQ)],
            xs.at[pl.ds(slot, n), :, :, pl.ds(C_AT + (NX - dx) * WQ, WQ)],
            x_s.at[i, dx - 1], x_r.at[i, dx - 1], dev(dx=dx),
        )

    def partial(k):
        return copy(sent.at[k], got.at[k], pp_s.at[k], pp_r.at[k], dev(ds=1))

    def slope_copy(k, first):
        ref = slopes.at[pl.ds(first, 2)]
        return copy(ref, ref, sl_s.at[k], sl_r.at[k], dev(ds=1))

    def late_of(slot):
        off = jnp.where(slot < 8, NZ - 1 - slot, jnp.where(slot == OWN, 0, slot - 7))
        return jnp.where(lax.rem(z + off, NZ) >= NZ // 2, 1, 0)

    def rows_of(slot):
        return xs[pl.ds(slot, 2)].reshape(ROWS, DH)

    for d in range(2):
        start(ring_first(d))
    for dy in range(1, NY):
        own_y(dy, y).start()

    def on_ring(k):
        @pl.when(k == 1)
        def _():
            for d in range(2):
                arrive(ring_first(d))

        @pl.when((k == 2) | (k == 3))
        def _():
            for d in range(2):
                arrive(ring_middle(d, k))

        @pl.when(k < 3)
        def _():
            for d in range(2):
                start(ring_middle(d, k + 1))

        @pl.when(k == 3)
        def _():
            for d in range(2):
                start(ring_last(d))

        @pl.when(k == STEPS)
        def _():
            for d in range(2):
                arrive(ring_last(d))

    def whole_or_not(k, d, do):
        first = 8 * d + 2 * (k - 1)
        if d == 0:
            do(first, 2)
        else:
            pl.when(k < STEPS)(lambda: do(first, 2))
            pl.when(k == STEPS)(lambda: do(first, 1))

    def step(k, carry):
        @pl.when(k <= STEPS)
        def _():
            on_ring(k)
            for d in range(2):

                def to_y(first, n, d=d):
                    for dy in range(1, NY):
                        relay_y(2 * k - 1 + d, dy, first, n, y).start()

                whole_or_not(k, d, to_y)

        @pl.when((k >= 2) & (k <= STEPS + 1))
        def _():
            j = k - 1
            for d in range(2):

                def y_to_x(first, n, d=d):
                    for dy in range(1, NY):
                        relay_y(2 * j - 1 + d, dy, first, n, wrap(y - dy, NY)).wait_recv()
                    for dx in range(1, NX):
                        relay_x(2 * j - 1 + d, dx, first, n).start()

                whole_or_not(j, d, y_to_x)

        @pl.when((k >= 3) & (k <= STEPS + 2))
        def _():
            j = k - 2
            for d in range(2):

                def from_x(first, n, d=d):
                    for dx in range(1, NX):
                        relay_x(2 * j - 1 + d, dx, first, n).wait_recv()

                whole_or_not(j, d, from_x)

            @pl.when(j == 1)
            def _():
                for c in h_copies:
                    c.wait()

            @pl.when(j == STEPS)
            def _():
                for dy in range(1, NY):
                    own_y(dy, wrap(y - dy, NY)).wait_recv()

            first = 2 * (j - 1)
            other = rows_of(first + 8 * (1 - s))
            sent[j - 1] = jnp.dot(other, hs[...], preferred_element_type=jnp.float32)
            partial(j - 1).start()
            own = rows_of(first + 8 * s)
            mine[j - 1] = jnp.dot(own, hs[...], preferred_element_type=jnp.float32)

        @pl.when(k >= 4)
        def _():
            j = k - 4
            first = 2 * j + 8 * s
            partial(j).wait_recv()

            def block(b, carry):
                slot = first + b // NY
                yb = lax.rem(b, NY)
                late = late_of(slot)
                rows = pl.ds(pl.multiple_of(b * 16, 16), 16)
                logits = mine[j, rows, :] + got[j, rows, :]
                small = jnp.exp(-jnp.abs(logits))
                soft = jnp.maximum(logits, 0.0) + jnp.log1p(small)
                pool[late, yb] += jnp.log1p(soft)
                top = jnp.where(logits >= 0.0, 1.0, small)
                slope = top / ((1.0 + small) * (1.0 + soft))
                slopes[slot, yb] = slope.astype(jnp.bfloat16)
                return carry

            lax.fori_loop(0, 2 * NY, block, 0)
            slope_copy(j, first).start()

        return carry

    lax.fori_loop(1, STEPS + 4, step, 0)

    lane = lax.broadcasted_iota(jnp.int32, (NQ, LANES), 1)
    row = lax.broadcasted_iota(jnp.int32, (NQ, LANES), 0)
    for c in inputs[2:]:
        c.wait()
    query = queries[...].astype(jnp.float32)
    terms = jnp.zeros((NQ, LANES), jnp.float32)
    for late in range(2):
        for yb in range(NY):
            for m in range(2):
                total = jnp.sum(pool[late, yb, m * 8 : (m + 1) * 8, :], axis=0, keepdims=True)
                term = jnp.sum(query * total, axis=1, keepdims=True)
                terms = jnp.where(lane == m * 8 + yb * 2 + late, term, terms)

    def transpose(c, carry):
        at = pl.multiple_of(c * LANES, LANES)
        block = xs[:, :, :, pl.ds(at, LANES)].reshape(TOKENS, LANES)
        xt[pl.ds(at, LANES), :] = block.T
        return carry

    ar0[...] = terms
    to_core = copy(ar0, ar1, a1_s, a1_r, dev(ds=1))
    to_core.start()
    to_core.wait_recv()
    chip = terms + ar1[...]
    ar0_xy = ar2.at[x * NY + y]
    ar2[x * NY + y] = chip

    def to_xy(i):
        return copy(ar0_xy, ar0_xy, a2_s.at[i], a2_r.at[i], dev(dx=i // NY, dy=lax.rem(i, NY)))

    def from_xy(i):
        ref = ar2.at[wrap(x - i // NY, NX) * NY + wrap(y - lax.rem(i, NY), NY)]
        return copy(ref, ref, a2_s.at[i], a2_r.at[i], dev())

    def start_xy(i, carry):
        to_xy(i).start()
        return carry

    def wait_xy(i, carry):
        from_xy(i).wait_recv()
        return carry

    lax.fori_loop(1, NX * NY, start_xy, 0)
    lax.fori_loop(0, 6, transpose, 0)
    lax.fori_loop(1, NX * NY, wait_xy, 0)
    plane = jnp.zeros((NQ, LANES), jnp.float32)
    for i in range(NX * NY):
        plane += ar2[i]
    ar3[z] = plane
    ar_z = ar3.at[z]

    def to_z(i):
        return copy(ar_z, ar_z, a3_s.at[i], a3_r.at[i], dev(dz=i))

    def from_z(i):
        ref = ar3.at[wrap(z - i, NZ)]
        return copy(ref, ref, a3_s.at[i], a3_r.at[i], dev())

    def start_z(i, carry):
        to_z(i).start()
        return carry

    def wait_z(i, carry):
        from_z(i).wait_recv()
        return carry

    lax.fori_loop(1, NZ, start_z, 0)
    lax.fori_loop(6, DH // LANES, transpose, 0)

    for d in range(2):
        for c in ring_first(d) + ring_middle(d, 2) + ring_middle(d, 3) + ring_last(d):
            c.wait_send()
    for o in range(1, NY):
        own_y(o, y).wait_send()
        for i in range(1, 2 * STEPS + 1):
            n = 1 if i == 2 * STEPS else 2
            relay_x(i, o, 0, n).wait_send()
            relay_y(i, o, 0, n, y).wait_send()
    for k in range(STEPS):
        slope_copy(k, 2 * k + 8 * (1 - s)).wait_recv()
        slope_copy(k, 2 * k + 8 * s).wait_send()
        partial(k).wait_send()
    for i, (dx, ds) in enumerate(near):
        p1(i, dx, ds, 0).wait_send()
    to_core.wait_send()

    def sent_xy(i, carry):
        to_xy(i).wait_send()
        return carry

    lax.fori_loop(1, NX * NY, sent_xy, 0)
    lax.fori_loop(1, NZ, wait_z, 0)
    whole = jnp.zeros((NQ, LANES), jnp.float32)
    for i in range(NZ):
        whole += ar3[i]

    masks = []
    first = jnp.int32(0)
    scores = jnp.zeros((NQ, LANES), jnp.float32)
    for d in range(NDOC):
        after = first + doc_spans[d]
        masks.append((lane >= first) & (lane < after))
        term = jnp.sum(jnp.where(masks[d], whole, 0.0), axis=1, keepdims=True)
        scores = jnp.where(lane == d, term, scores)
        first = after
    scores = scores * (1.0 / (math.sqrt(VOCAB) * SPAN))
    valid = lane < NDOC
    row_top = jnp.max(jnp.where(valid, scores, -jnp.inf), axis=1, keepdims=True)
    total = jnp.sum(jnp.where(valid, jnp.exp(scores - row_top), 0.0), axis=1, keepdims=True)
    log_total = row_top + jnp.log(total)
    picks = jnp.zeros((NQ, LANES), jnp.float32)
    for q in range(NQ):
        picks = jnp.where((row == q) & (lane == labels[q]), 1.0, picks)
    picked = jnp.sum(scores * picks, axis=1, keepdims=True)
    loss[...] = jnp.sum(log_total - picked, axis=0, keepdims=True)
    grad = jnp.where(valid, jnp.exp(scores - log_total), 0.0) - picks
    grad = grad * (1.0 / math.sqrt(TOKENS))
    by_span = jnp.zeros((NQ, LANES), jnp.float32)
    for d in range(NDOC):
        column = jnp.sum(jnp.where(lane == d, grad, 0.0), axis=1, keepdims=True)
        by_span = jnp.where(masks[d], column, by_span)
    for i in range(SPANS):
        m, yb, late = i // 8, i // 2 % NY, i % 2
        spg[late, 2 * yb + m : 2 * yb + m + 1, :] = jnp.sum(
            by_span[:, i : i + 1] * query, axis=0, keepdims=True
        )

    def to_lg(slot, carry):
        factors = spg[late_of(slot)]
        for yb in range(NY):
            slope = slopes[slot, yb].astype(jnp.float32)
            parts = [
                slope[m * 8 : (m + 1) * 8] * factors[2 * yb + m : 2 * yb + m + 1] for m in range(2)
            ]
            at = pl.multiple_of(slot * 64 + yb * 16, 16)
            lg[pl.ds(at, 16), :] = jnp.concatenate(parts, axis=0).astype(jnp.bfloat16)
        return carry

    lax.fori_loop(0, NZ, to_lg, 0)

    def out_copy(b):
        here = pl.ds(pl.multiple_of(b * WQ, WQ), WQ)
        quarter = C_AT // WQ + wrap(x + b - C_AT // WQ, NX)
        at = pl.multiple_of(jnp.where(b < C_AT // WQ, b, quarter) * WQ, WQ)
        return pltpu.make_async_copy(outs.at[here], out.at[pl.ds(at, WQ)], o_sem.at[b])

    def to_out(b, carry):
        here = pl.ds(pl.multiple_of(b * WQ, WQ), WQ)
        block = jnp.dot(xt[here, :], lg[...], preferred_element_type=jnp.float32)
        outs[here, :] = block.astype(jnp.bfloat16)
        out_copy(b).start()
        return carry

    lax.fori_loop(0, DH // WQ, to_out, 0)

    def sent_z(i, carry):
        to_z(i).wait_send()
        return carry

    lax.fori_loop(1, NZ, sent_z, 0)

    def out_wait(b, carry):
        out_copy(b).wait()
        return carry

    lax.fori_loop(0, DH // WQ, out_wait, 0)


def shards(hidden, gain, head, queries, doc_spans, labels):
    dma = pltpu.SemaphoreType.DMA
    f32, bf16 = jnp.float32, jnp.bfloat16
    vmem = pl.BlockSpec(memory_space=pltpu.VMEM)
    hbm = pl.BlockSpec(memory_space=pltpu.HBM)
    grad_head, loss = pl.pallas_call(
        kernel,
        name="splade_head",
        out_shape=(
            jax.ShapeDtypeStruct((DH, V_DEV), bf16),
            jax.ShapeDtypeStruct((1, 1), f32),
        ),
        in_specs=[hbm] * 6,
        out_specs=(hbm, vmem),
        scratch_shapes=[
            pltpu.VMEM((1, 2, D), bf16),
            pltpu.VMEM((1, D), f32),
            pltpu.VMEM((NQ, V_DEV), bf16),
            pltpu.SMEM((NDOC,), jnp.int32),
            pltpu.SMEM((NQ,), jnp.int32),
            pltpu.VMEM((2, 2, 16, LANES), f32),
            pltpu.VMEM((16, 16, LANES), f32),
            pltpu.VMEM((NZ, NY, 16, DH), bf16),
            pltpu.VMEM((DH, V_DEV), bf16),
            pltpu.VMEM((STEPS, ROWS, V_DEV), f32),
            pltpu.VMEM((STEPS, ROWS, V_DEV), f32),
            pltpu.VMEM((STEPS, ROWS, V_DEV), f32),
            pltpu.VMEM((NZ, NY, 16, V_DEV), bf16),
            pltpu.VMEM((2, NY, 16, V_DEV), f32),
            pltpu.VMEM((DH, TOKENS), bf16),
            pltpu.VMEM((TOKENS, V_DEV), bf16),
            pltpu.VMEM((DH, V_DEV), bf16),
            pltpu.VMEM((2, 8, V_DEV), f32),
            pltpu.VMEM((NQ, LANES), f32),
            pltpu.VMEM((NQ, LANES), f32),
            pltpu.VMEM((NX * NY, NQ, LANES), f32),
            pltpu.VMEM((NZ, NQ, LANES), f32),
            dma((5,)), dma((5,)), dma((DH // WQ,)),
            dma((7,)), dma((7,)),
            dma((9, 3)), dma((9, 3)),
            dma((20,)), dma((20,)),
            dma((9, 3)), dma((9, 3)),
            dma((STEPS,)), dma((STEPS,)),
            dma((STEPS,)), dma((STEPS,)),
            dma, dma,
            dma((16,)), dma((16,)),
            dma((16,)), dma((16,)),
        ],
        compiler_params=pltpu.CompilerParams(
            collective_id=0, has_side_effects=True, vmem_limit_bytes=67_000_000
        ),
    )(hidden, gain.reshape(1, D), head, queries, doc_spans, labels)
    return (grad_head, loss.reshape(()))


def solution(mesh):
    return jax.shard_map(
        shards,
        mesh=mesh,
        in_specs=(
            P("segment", ("dp", "mp"), None),
            P(),
            P("segment", ("dp", "mp")),
            P(None, ("dp", "mp")),
            P(),
            P(),
        ),
        out_specs=(P("segment", ("dp", "mp")), P()),
        check_vma=False,
    )
```

```python
import functools
import math

import jax
import jax.numpy as jnp
from jax import lax
from jax.experimental import pallas as pl
from jax.experimental.pallas import tpu as pltpu
from jax.sharding import PartitionSpec as P

MESH = pl.DeviceIdType.MESH
NX, NY, NZ = 4, 4, 16
V_DEV = 512
NDOC = 8
NQ = 8
SPANS = 16
ROWS = 128
SPAN = 64
VOCAB = 131072
TOKENS = 1024
D = 4096
DH = D // 2
LANES = 128

WB, WQ = 1024, 256
WHOLE = (0, WB + WQ)
HALVES = ((0, 640), (640, WB + WQ - 640))
C_AT = WB
assert C_AT + 4 * WQ == DH

OWN = 15
STEPS = 4


def around(at, by, n):
    by %= n
    if by == 0:
        return at
    return jnp.where(at >= n - by, at + (by - n), at + by)


def kernel(
    hidden_at, gain_at, head, queries_at, doc_spans_at, labels_at,
    out, loss,
    hidden, gain, queries, doc_spans, labels,
    ysend, yland, xs, hs, mine, sent, got, slopes, pool, xt, lg, outs, spg,
    ar0, ar1, ar2, ar3,
    in_sem, h_sem, o_sem,
    p1_s, p1_r, y_s, y_r, r_s, r_r, x_s, x_r, pp_s, pp_r, sl_s, sl_r,
    a1_s, a1_r, a2_s, a2_r, a3_s, a3_r,
):
    x = lax.axis_index("mp")
    s = lax.axis_index("segment")
    dp = lax.axis_index("dp")
    y = dp // NZ
    z = lax.rem(dp, NZ)

    xs_of = [around(x, i, NX) for i in range(NX)]
    ys_of = [around(y, i, NY) for i in range(NY)]
    zs_of = [around(z, i, NZ) for i in range(NZ)]
    ss_of = [s, 1 - s]

    def dev(dx=0, dy=0, dz=0, ds=0):
        return (ys_of[dy % NY] * NZ + zs_of[dz % NZ], ss_of[ds], xs_of[dx % NX])

    def copy(src, dst, s_sem, r_sem, device):
        return pltpu.make_async_remote_copy(
            src, dst, s_sem, r_sem, device, device_id_type=MESH
        )

    inputs = [
        pltpu.make_async_copy(a, b, in_sem.at[i])
        for i, (a, b) in enumerate(
            ((hidden_at, hidden), (gain_at, gain), (queries_at, queries),
             (doc_spans_at, doc_spans), (labels_at, labels))
        )
    ]
    for c in inputs:
        c.start()

    near = [(dx, ds) for dx in range(NX) for ds in range(2) if dx or ds]
    barrier = pltpu.get_barrier_semaphore()
    peers = [dev(dx=dx, ds=ds) for dx, ds in near]
    peers += [dev(dy=dy) for dy in range(1, NY)]
    peers += [dev(dz=dz) for dz in (1, 2, -1, -2)]
    for p in peers:
        pl.semaphore_signal(barrier, inc=1, device_id=p, device_id_type=MESH)

    h_copies = [pltpu.make_async_copy(head.at[pl.ds(0, C_AT)], hs.at[pl.ds(0, C_AT)], h_sem.at[0])]
    for r in range(NX):
        at = pl.multiple_of(C_AT + xs_of[r] * WQ, WQ)
        h_copies.append(
            pltpu.make_async_copy(
                head.at[pl.ds(at, WQ)], hs.at[pl.ds(C_AT + r * WQ, WQ)], h_sem.at[1 + r]
            )
        )

    inputs[0].wait()
    inputs[1].wait()
    values = hidden[0].astype(jnp.float32)
    mean_sq = jnp.mean(values * values, axis=-1, keepdims=True)
    normed = (values * lax.rsqrt(mean_sq + 1e-05) * gain[...]).astype(jnp.bfloat16)
    normed = normed.astype(jnp.float32)
    for k in range(D // LANES):
        ysend[k // 16, :, k % 16, :] = normed[:, k * LANES : (k + 1) * LANES]

    pl.semaphore_wait(barrier, len(peers))

    def p1(i, dx, ds, landing):
        return copy(
            ysend.at[ss_of[ds]],
            yland.at[pl.ds(landing * 2, 2)],
            p1_s.at[i], p1_r.at[i], dev(dx=dx, ds=ds),
        )

    for i, (dx, ds) in enumerate(near):
        p1(i, dx, ds, s * NX + x).start()
    for c in h_copies:
        c.start()
    yland[pl.ds((s * NX + x) * 2, 2)] = ysend[s]
    pool[...] = jnp.zeros_like(pool)
    for i, (dx, ds) in enumerate(near):
        p1(i, dx, ds, ss_of[ds] * NX + xs_of[-dx % NX]).wait_recv()
    for k in range(C_AT // LANES):
        xs[OWN, y, :, k * LANES : (k + 1) * LANES] = yland[:, k, :].astype(jnp.bfloat16)
    for xx in range(NX):

        @pl.when(x == xx)
        def _():
            for r in range(NX):
                for h in range(WQ // LANES):
                    k = (C_AT + (xx + r) % NX * WQ) // LANES + h
                    at = C_AT + r * WQ + h * LANES
                    xs[OWN, y, :, at : at + LANES] = yland[:, k, :].astype(jnp.bfloat16)

    def ring_copy(k, d, piece, src, dst, n, hops, columns=WHOLE):
        a, b = (xs.at[pl.ds(i, n), y, :, pl.ds(*columns)] for i in (src, dst))
        at = 4 * k + 2 * d + piece
        return copy(a, b, r_s.at[at], r_r.at[at], dev(dz=hops if d == 0 else -hops))

    def ring_first(d):
        return [ring_copy(1, d, i, OWN, 8 * d + i, 1, 1 + i) for i in range(2)]

    def ring_middle(d, k):
        at = 8 * d + 2 * (k - 1)
        return [ring_copy(k, d, 0, at - 2, at, 2, 2)]

    def ring_last(d):
        return [
            ring_copy(STEPS, d, 0, 8 * d + 4, 8 * d + 6, 1, 2),
            ring_copy(STEPS, d, 1, 8 * d + 5, 7, 1, 2, HALVES[d]),
        ]

    def start(copies):
        for c in copies:
            c.start()

    def arrive(copies):
        for c in copies:
            c.wait_recv()

    def own_y(dy, yb):
        ref = xs.at[OWN, yb]
        return copy(ref, ref, y_s.at[0, dy - 1], y_r.at[0, dy - 1], dev(dy=dy))

    def relay_y(i, dy, slot, n, yb):
        ref = xs.at[pl.ds(slot, n), yb, :, pl.ds(*WHOLE)]
        return copy(ref, ref, y_s.at[i, dy - 1], y_r.at[i, dy - 1], dev(dy=dy))

    def relay_x(i, dx, slot, n):
        return copy(
            xs.at[pl.ds(slot, n), :, :, pl.ds(C_AT, WQ)],
            xs.at[pl.ds(slot, n), :, :, pl.ds(C_AT + (NX - dx) * WQ, WQ)],
            x_s.at[i, dx - 1], x_r.at[i, dx - 1], dev(dx=dx),
        )

    def partial(k):
        return copy(sent.at[k], got.at[k], pp_s.at[k], pp_r.at[k], dev(ds=1))

    def slope_copy(k, first):
        ref = slopes.at[pl.ds(first, 2)]
        return copy(ref, ref, sl_s.at[k], sl_r.at[k], dev(ds=1))

    def late_of(slot):
        off = jnp.where(slot < 8, NZ - 1 - slot, jnp.where(slot == OWN, 0, slot - 7))
        return jnp.where(lax.rem(z + off, NZ) >= NZ // 2, 1, 0)

    def term(slot, at, end):
        rows = xs[pl.ds(slot, 2), :, :, at:end].reshape(ROWS, end - at)
        return jnp.dot(rows, hs[at:end, :], preferred_element_type=jnp.float32)

    for d in range(2):
        start(ring_first(d))
    for dy in range(1, NY):
        own_y(dy, y).start()

    def on_ring(k):
        @pl.when(k == 1)
        def _():
            for d in range(2):
                arrive(ring_first(d))

        @pl.when((k == 2) | (k == 3))
        def _():
            for d in range(2):
                arrive(ring_middle(d, k))

        @pl.when(k < 3)
        def _():
            for d in range(2):
                start(ring_middle(d, k + 1))

        @pl.when(k == 3)
        def _():
            for d in range(2):
                start(ring_last(d))

        @pl.when(k == STEPS)
        def _():
            for d in range(2):
                arrive(ring_last(d))

    def whole_or_not(k, d, do):
        first = 8 * d + 2 * (k - 1)
        if d == 0:
            do(first, 2)
        else:
            pl.when(k < STEPS)(lambda: do(first, 2))
            pl.when(k == STEPS)(lambda: do(first, 1))

    def step(k, carry):
        @pl.when(k <= STEPS)
        def _():
            on_ring(k)
            for d in range(2):

                def to_y(first, n, d=d):
                    for dy in range(1, NY):
                        relay_y(2 * k - 1 + d, dy, first, n, y).start()

                whole_or_not(k, d, to_y)

        @pl.when((k >= 2) & (k <= STEPS + 1))
        def _():
            j = k - 1
            for d in range(2):

                def y_to_x(first, n, d=d):
                    for dy in range(1, NY):
                        relay_y(2 * j - 1 + d, dy, first, n, ys_of[-dy % NY]).wait_recv()
                    for dx in range(1, NX):
                        relay_x(2 * j - 1 + d, dx, first, n).start()

                whole_or_not(j, d, y_to_x)

            @pl.when(j == 1)
            def _():
                for c in h_copies:
                    c.wait()

            @pl.when(j == STEPS)
            def _():
                for dy in range(1, NY):
                    own_y(dy, ys_of[-dy % NY]).wait_recv()

            first = 2 * (j - 1)
            sent[j - 1] = term(first + 8 * (1 - s), 0, WB + WQ)
            mine[j - 1] = term(first + 8 * s, 0, WB + WQ)

        @pl.when((k >= 3) & (k <= STEPS + 2))
        def _():
            j = k - 2
            for d in range(2):

                def from_x(first, n, d=d):
                    for dx in range(1, NX):
                        relay_x(2 * j - 1 + d, dx, first, n).wait_recv()

                whole_or_not(j, d, from_x)

            first = 2 * (j - 1)
            sent[j - 1] += term(first + 8 * (1 - s), WB + WQ, DH)
            partial(j - 1).start()
            mine[j - 1] += term(first + 8 * s, WB + WQ, DH)

        @pl.when(k >= 4)
        def _():
            j = k - 4
            first = 2 * j + 8 * s
            partial(j).wait_recv()

            for o in range(2):
                slot = first + o
                late = late_of(slot)

                def block(yb, carry, o=o, slot=slot, late=late):
                    rows = pl.ds(pl.multiple_of(o * 64 + yb * 16, 16), 16)
                    logits = mine[j, rows, :] + got[j, rows, :]
                    small = jnp.exp(-jnp.abs(logits))
                    soft = jnp.maximum(logits, 0.0) + jnp.log1p(small)
                    pool[late, yb] += jnp.log1p(soft)
                    top = jnp.where(logits >= 0.0, 1.0, small)
                    slope = top / ((1.0 + small) * (1.0 + soft))
                    slopes[slot, yb] = slope.astype(jnp.bfloat16)
                    return carry

                lax.fori_loop(0, NY, block, 0)
            slope_copy(j, first).start()

        return carry

    lax.fori_loop(1, STEPS + 4, step, 0)

    lane = lax.broadcasted_iota(jnp.int32, (NQ, LANES), 1)
    row = lax.broadcasted_iota(jnp.int32, (NQ, LANES), 0)
    for c in inputs[2:]:
        c.wait()
    query = queries[...].astype(jnp.float32)
    terms = jnp.zeros((NQ, LANES), jnp.float32)
    for late in range(2):
        for yb in range(NY):
            for m in range(2):
                total = jnp.sum(pool[late, yb, m * 8 : (m + 1) * 8, :], axis=0, keepdims=True)
                term = jnp.sum(query * total, axis=1, keepdims=True)
                terms = jnp.where(lane == m * 8 + yb * 2 + late, term, terms)

    def transpose(c, carry):
        at = pl.multiple_of(c * LANES, LANES)
        block = xs[:, :, :, pl.ds(at, LANES)].reshape(TOKENS, LANES)
        xt[pl.ds(at, LANES), :] = block.T
        return carry

    ar0[...] = terms
    to_core = copy(ar0, ar1, a1_s, a1_r, dev(ds=1))
    to_core.start()
    to_core.wait_recv()
    chip = terms + ar1[...]
    ar0_xy = ar2.at[x * NY + y]
    ar2[x * NY + y] = chip

    plane_peers = [(dx, dy) for dx in range(NX) for dy in range(NY) if dx or dy]

    def to_xy(dx, dy):
        i = dx * NY + dy
        return copy(ar0_xy, ar0_xy, a2_s.at[i], a2_r.at[i], dev(dx=dx, dy=dy))

    def from_xy(dx, dy):
        i = dx * NY + dy
        ref = ar2.at[xs_of[-dx % NX] * NY + ys_of[-dy % NY]]
        return copy(ref, ref, a2_s.at[i], a2_r.at[i], dev(dx=dx, dy=dy))

    for dx, dy in plane_peers:
        to_xy(dx, dy).start()
    lax.fori_loop(0, 6, transpose, 0)
    for dx, dy in plane_peers:
        from_xy(dx, dy).wait_recv()
    plane = jnp.zeros((NQ, LANES), jnp.float32)
    for i in range(NX * NY):
        plane += ar2[i]
    ar3[z] = plane
    ar_z = ar3.at[z]

    def to_z(i):
        return copy(ar_z, ar_z, a3_s.at[i], a3_r.at[i], dev(dz=i))

    def from_z(i):
        ref = ar3.at[zs_of[-i % NZ]]
        return copy(ref, ref, a3_s.at[i], a3_r.at[i], dev(dz=i))

    for i in range(1, NZ):
        to_z(i).start()
    lax.fori_loop(6, DH // LANES, transpose, 0)

    for d in range(2):
        for c in ring_first(d) + ring_middle(d, 2) + ring_middle(d, 3) + ring_last(d):
            c.wait_send()
    for o in range(1, NY):
        own_y(o, y).wait_send()
        for i in range(1, 2 * STEPS + 1):
            n = 1 if i == 2 * STEPS else 2
            relay_x(i, o, 0, n).wait_send()
            relay_y(i, o, 0, n, y).wait_send()
    for k in range(STEPS):
        slope_copy(k, 2 * k + 8 * (1 - s)).wait_recv()
        slope_copy(k, 2 * k + 8 * s).wait_send()
        partial(k).wait_send()
    for i, (dx, ds) in enumerate(near):
        p1(i, dx, ds, 0).wait_send()
    to_core.wait_send()

    for dx, dy in plane_peers:
        to_xy(dx, dy).wait_send()
    for i in range(1, NZ):
        from_z(i).wait_recv()
    whole = jnp.zeros((NQ, LANES), jnp.float32)
    for i in range(NZ):
        whole += ar3[i]

    masks = []
    first = jnp.int32(0)
    scores = jnp.zeros((NQ, LANES), jnp.float32)
    for d in range(NDOC):
        after = first + doc_spans[d]
        masks.append((lane >= first) & (lane < after))
        term = jnp.sum(jnp.where(masks[d], whole, 0.0), axis=1, keepdims=True)
        scores = jnp.where(lane == d, term, scores)
        first = after
    scores = scores * (1.0 / (math.sqrt(VOCAB) * SPAN))
    valid = lane < NDOC
    row_top = jnp.max(jnp.where(valid, scores, -jnp.inf), axis=1, keepdims=True)
    total = jnp.sum(jnp.where(valid, jnp.exp(scores - row_top), 0.0), axis=1, keepdims=True)
    log_total = row_top + jnp.log(total)
    picks = jnp.zeros((NQ, LANES), jnp.float32)
    for q in range(NQ):
        picks = jnp.where((row == q) & (lane == labels[q]), 1.0, picks)
    picked = jnp.sum(scores * picks, axis=1, keepdims=True)
    loss[...] = jnp.sum(log_total - picked, axis=0, keepdims=True)
    grad = jnp.where(valid, jnp.exp(scores - log_total), 0.0) - picks
    grad = grad * (1.0 / math.sqrt(TOKENS))
    by_span = jnp.zeros((NQ, LANES), jnp.float32)
    for d in range(NDOC):
        column = jnp.sum(jnp.where(lane == d, grad, 0.0), axis=1, keepdims=True)
        by_span = jnp.where(masks[d], column, by_span)
    for i in range(SPANS):
        m, yb, late = i // 8, i // 2 % NY, i % 2
        spg[late, 2 * yb + m : 2 * yb + m + 1, :] = jnp.sum(
            by_span[:, i : i + 1] * query, axis=0, keepdims=True
        )

    def to_lg(slot, carry):
        factors = spg[late_of(slot)]
        for yb in range(NY):
            slope = slopes[slot, yb].astype(jnp.float32)
            parts = [
                slope[m * 8 : (m + 1) * 8] * factors[2 * yb + m : 2 * yb + m + 1] for m in range(2)
            ]
            at = pl.multiple_of(slot * 64 + yb * 16, 16)
            lg[pl.ds(at, 16), :] = jnp.concatenate(parts, axis=0).astype(jnp.bfloat16)
        return carry

    lax.fori_loop(0, NZ, to_lg, 0)

    def out_copy(b):
        here = pl.ds(pl.multiple_of(b * WQ, WQ), WQ)
        quarter = C_AT // WQ + lax.rem(x + jnp.maximum(b - C_AT // WQ, 0), NX)
        at = pl.multiple_of(jnp.where(b < C_AT // WQ, b, quarter) * WQ, WQ)
        return pltpu.make_async_copy(outs.at[here], out.at[pl.ds(at, WQ)], o_sem.at[b])

    def to_out(b, carry):
        here = pl.ds(pl.multiple_of(b * WQ, WQ), WQ)
        block = jnp.dot(xt[here, :], lg[...], preferred_element_type=jnp.float32)
        outs[here, :] = block.astype(jnp.bfloat16)
        out_copy(b).start()
        return carry

    lax.fori_loop(0, DH // WQ, to_out, 0)

    for i in range(1, NZ):
        to_z(i).wait_send()

    def out_wait(b, carry):
        out_copy(b).wait()
        return carry

    lax.fori_loop(0, DH // WQ, out_wait, 0)


def shards(hidden, gain, head, queries, doc_spans, labels):
    dma = pltpu.SemaphoreType.DMA
    f32, bf16 = jnp.float32, jnp.bfloat16
    vmem = pl.BlockSpec(memory_space=pltpu.VMEM)
    hbm = pl.BlockSpec(memory_space=pltpu.HBM)
    grad_head, loss = pl.pallas_call(
        kernel,
        name="splade_head",
        out_shape=(
            jax.ShapeDtypeStruct((DH, V_DEV), bf16),
            jax.ShapeDtypeStruct((1, 1), f32),
        ),
        in_specs=[hbm] * 6,
        out_specs=(hbm, vmem),
        scratch_shapes=[
            pltpu.VMEM((1, 2, D), bf16),
            pltpu.VMEM((1, D), f32),
            pltpu.VMEM((NQ, V_DEV), bf16),
            pltpu.SMEM((NDOC,), jnp.int32),
            pltpu.SMEM((NQ,), jnp.int32),
            pltpu.VMEM((2, 2, 16, LANES), f32),
            pltpu.VMEM((16, 16, LANES), f32),
            pltpu.VMEM((NZ, NY, 16, DH), bf16),
            pltpu.VMEM((DH, V_DEV), bf16),
            pltpu.VMEM((STEPS, ROWS, V_DEV), f32),
            pltpu.VMEM((STEPS, ROWS, V_DEV), f32),
            pltpu.VMEM((STEPS, ROWS, V_DEV), f32),
            pltpu.VMEM((NZ, NY, 16, V_DEV), bf16),
            pltpu.VMEM((2, NY, 16, V_DEV), f32),
            pltpu.VMEM((DH, TOKENS), bf16),
            pltpu.VMEM((TOKENS, V_DEV), bf16),
            pltpu.VMEM((DH, V_DEV), bf16),
            pltpu.VMEM((2, 8, V_DEV), f32),
            pltpu.VMEM((NQ, LANES), f32),
            pltpu.VMEM((NQ, LANES), f32),
            pltpu.VMEM((NX * NY, NQ, LANES), f32),
            pltpu.VMEM((NZ, NQ, LANES), f32),
            dma((5,)), dma((5,)), dma((DH // WQ,)),
            dma((7,)), dma((7,)),
            dma((9, 3)), dma((9, 3)),
            dma((20,)), dma((20,)),
            dma((9, 3)), dma((9, 3)),
            dma((STEPS,)), dma((STEPS,)),
            dma((STEPS,)), dma((STEPS,)),
            dma, dma,
            dma((16,)), dma((16,)),
            dma((16,)), dma((16,)),
        ],
        compiler_params=pltpu.CompilerParams(
            collective_id=0, has_side_effects=True, vmem_limit_bytes=67_000_000
        ),
    )(hidden, gain.reshape(1, D), head, queries, doc_spans, labels)
    return (grad_head, loss.reshape(()))


def solution(mesh):
    return jax.shard_map(
        shards,
        mesh=mesh,
        in_specs=(
            P("segment", ("dp", "mp"), None),
            P(),
            P("segment", ("dp", "mp")),
            P(None, ("dp", "mp")),
            P(),
            P(),
        ),
        out_specs=(P("segment", ("dp", "mp")), P()),
        check_vma=False,
    )
```
